32 devices in a mesh: section: 4 (over y, core), tensor: 8 (over z, x).
Axes of the slice: x: 2, y: 2, z: 4, core: 2. Of those that a mesh axis runs over, the one named last changes fastest.
Arguments:
- inputs: bfloat16 [2, 256, 12288], P(None, 'section', 'tensor'), may hold values from -6 to 6
- cotangent: bfloat16 [2, 256, 12288], P(None, 'section', 'tensor'), may hold values from -1.5 to 1.5
- up_weight: bfloat16 [12288, 24576], P('tensor', 'section'), may hold values from -0.04059494 to 0.067658235
- down_weight: bfloat16 [24576, 12288], P('section', 'tensor'), may hold values from -0.0390625 to 0.0390625
- norm_gain: float32 [12288], P('tensor'), may hold values from 0.25 to 2.8
Outputs:
- states: bfloat16 [2, 256, 12288], P(None, 'section', 'tensor')
- input_grads: bfloat16 [2, 256, 12288], P(None, 'section', 'tensor')
- grad_up: bfloat16 [12288, 24576], P('tensor', 'section')
- grad_down: bfloat16 [24576, 12288], P('section', 'tensor')
- grad_gain: float32 [12288], P('tensor')
The draws below stay inside these ranges and needn't reach their ends.
All inputs are finite; a program needn't handle non-finite values.
Results may differ from the reference program's by a relative error of at most 0.03.
Values may be sent and summed in bfloat16 or wider, within the bound.
A program may use at most 192 MiB of HBM per device.

```python
import jax
import jax.numpy as jnp
from jax import lax

D = 12288
HID = 24576
R = 256
M = 2
N_SECTION = 4
N_TENSOR = 8


def draw_up_weight(key, part):
    inner_key = jax.random.fold_in(key, 11)
    noise = jnp.clip(jax.random.normal(inner_key, (D, HID), jnp.float32), -6.0, 6.0)
    values = (noise + 1.5) * float(D) ** (-0.5)
    return values.astype(jnp.bfloat16)


def draw_norm_gain(key, part):
    inner_key = jax.random.fold_in(key, 23)
    ramp = jnp.arange(D, dtype=jnp.float32) / float(D - 1)
    rough = jax.random.uniform(inner_key, (D,), jnp.float32, 0.8, 1.2)
    values = (0.5 + 1.4 * ramp) * rough
    return values.astype(jnp.float32)


def shard_levels(rng, dims, shards, low, high):
    level = 1.0
    for dim, blocks in shards:
        heights = jax.random.uniform(jax.random.fold_in(jax.random.fold_in(rng, 6), dim), (blocks,), jnp.float32, low / len(shards), high / len(shards))
        level = level * jnp.repeat(jnp.exp(heights), dims[dim] // blocks).reshape((-1,) + (1,) * (len(dims) - 1 - dim))
    return level


def scatter_about(rng, shape, width, reach, pieces=(), held_as=jnp.bfloat16):
    values = width * jax.random.normal(rng, shape, jnp.float32)
    if pieces:
        values = values * shard_levels(rng, shape, pieces, -0.22, 0.18)
    return jnp.clip(values, -reach, reach).astype(held_as)


def setup_inputs(seed: int = 0) -> dict:
    arg_keys = jax.random.split(jax.random.key(seed), 6)
    return {
        "inputs": scatter_about(arg_keys[0], (M, R, D), 1.0, 6.0, ((1, 4), (2, 8))),
        "cotangent": scatter_about(arg_keys[1], (M, R, D), 0.25, 1.5, ((1, 4), (2, 8))),
        "up_weight": draw_up_weight(jax.random.fold_in(arg_keys[5], 71), 0),
        "down_weight": scatter_about(arg_keys[3], (HID, D), HID ** -0.5, 0.0390625, ((0, 4), (1, 8))),
        "norm_gain": draw_norm_gain(jax.random.fold_in(arg_keys[5], 71), 0),
    }


norm_eps = 1e-05
gelu_c = 0.7978845608
cubic_c = 0.044715

def gelu_tanh(values):
    inner_arg = gelu_c * (values + cubic_c * values * values * values)
    return 0.5 * values * (1.0 + jnp.tanh(inner_arg))

def gelu_slope(values):
    tanh_value = jnp.tanh(gelu_c * (values + cubic_c * values * values * values))
    return 0.5 * (1.0 + tanh_value) + 0.5 * values * (1.0 - tanh_value * tanh_value) * gelu_c * (1.0 + 3.0 * cubic_c * values * values)

def block_sum(left, right, blocks):
    span = left.shape[1] // blocks
    total = jnp.zeros((left.shape[0], right.shape[1]), jnp.float32)
    for block_num in range(blocks):
        part = jnp.dot(left[:, block_num * span:(block_num + 1) * span], right[block_num * span:(block_num + 1) * span], preferred_element_type=jnp.float32)
        rounded = lax.optimization_barrier(part.astype(jnp.bfloat16))
        total = total + rounded.astype(jnp.float32)
    return total

def reference(inputs, cotangent, up_weight, down_weight, norm_gain):
    row_count = M * R
    layer_in = inputs.reshape(row_count, D)
    in_float = layer_in.astype(jnp.float32)
    row_mean = lax.optimization_barrier(jnp.sum(in_float, axis=1, keepdims=True)) / D
    row_squares = lax.optimization_barrier(jnp.sum(in_float * in_float, axis=1, keepdims=True)) / D
    row_scale = lax.rsqrt(row_squares - row_mean * row_mean + norm_eps)
    centred = (in_float - row_mean) * row_scale
    normed = (centred * norm_gain).astype(jnp.bfloat16)
    pre_act = block_sum(normed, up_weight, N_TENSOR)
    hidden = gelu_tanh(pre_act).astype(jnp.bfloat16)
    states = (in_float + block_sum(hidden, down_weight, N_SECTION)).astype(jnp.bfloat16).reshape(M, R, D)
    grad_out = cotangent.reshape(row_count, D)
    grad_down = jnp.dot(hidden.T, grad_out, preferred_element_type=jnp.float32).astype(jnp.bfloat16)
    grad_hidden = block_sum(grad_out, down_weight.T, N_TENSOR)
    grad_pre = (grad_hidden * gelu_slope(pre_act)).astype(jnp.bfloat16)
    grad_up = jnp.dot(normed.T, grad_pre, preferred_element_type=jnp.float32).astype(jnp.bfloat16)
    grad_normed = block_sum(grad_pre, up_weight.T, N_SECTION)
    grad_gain = lax.optimization_barrier(jnp.sum(grad_normed * centred, axis=0))
    grad_centred = grad_normed * norm_gain
    mean_first = lax.optimization_barrier(jnp.sum(grad_centred, axis=1, keepdims=True)) / D
    mean_second = lax.optimization_barrier(jnp.sum(grad_centred * centred, axis=1, keepdims=True)) / D
    grad_in = (grad_out.astype(jnp.float32) + row_scale * (grad_centred - mean_first - centred * mean_second)).astype(jnp.bfloat16)
    return (states, grad_in.reshape(M, R, D), grad_up, grad_down, grad_gain)
```

```python
import jax
import jax.numpy as jnp
from jax import lax
from jax.sharding import PartitionSpec as P

D = 12288


norm_eps = 1e-05
gelu_c = 0.7978845608
cubic_c = 0.044715


def gelu_tanh(values):
    inner_arg = gelu_c * (values + cubic_c * values * values * values)
    return 0.5 * values * (1.0 + jnp.tanh(inner_arg))


def gelu_slope(values):
    tanh_value = jnp.tanh(gelu_c * (values + cubic_c * values * values * values))
    return 0.5 * (1.0 + tanh_value) + 0.5 * values * (1.0 - tanh_value * tanh_value) * gelu_c * (
        1.0 + 3.0 * cubic_c * values * values
    )


def ring_pairs(count, step):
    ring = list(range(0, count, 2)) + list(range(count - 1, 0, -2))
    return [(ring[i], ring[(i + step) % count]) for i in range(count)]


def ring_place(count):
    index = lax.axis_index("tensor")
    return jnp.where(index % 2 == 0, index // 2, count - 1 - index // 2)


def ring_reduce_scatter(partial, step):
    count = lax.axis_size("tensor")
    place = ring_place(count)
    rows = partial.shape[0] // count
    pairs = ring_pairs(count, step)

    def own(owner):
        owner = lax.rem(owner + 2 * count, count)
        return lax.dynamic_slice(partial, (owner * rows, 0), (rows, partial.shape[1]))

    held = own(place - step)
    for hop in range(count - 1):
        arrived = lax.ppermute(held, "tensor", pairs)
        total = arrived.astype(jnp.float32) + own(place - step * (2 + hop)).astype(jnp.float32)
        held = total.astype(jnp.bfloat16)
    return total


def ring_gather(blocks):
    count = lax.axis_size("tensor")
    place = ring_place(count)
    rows, half = blocks[0].shape
    whole = jnp.zeros((rows * count, 2 * half), jnp.bfloat16)
    held = list(blocks)
    for hop in range(count):
        for way, step in enumerate((1, -1)):
            owner = lax.rem(place - step * hop + count, count)
            whole = lax.dynamic_update_slice(whole, held[way], (owner * rows, way * half))
        if hop < count - 1:
            held = [
                lax.ppermute(held[way], "tensor", ring_pairs(count, step))
                for way, step in enumerate((1, -1))
            ]
    return whole


def per_device(inputs, cotangent, up_weight, down_weight, norm_gain):
    micro_count = inputs.shape[0]
    local_rows = inputs.shape[1]
    width = inputs.shape[2]
    hid_width = up_weight.shape[1]
    half = hid_width // 2
    section_count = lax.axis_size("section")
    row_total = local_rows * section_count
    flat_rows = micro_count * row_total
    in_float = inputs.astype(jnp.float32)
    grad_all = lax.all_gather(cotangent, "section", axis=1, tiled=True).reshape(flat_rows, width)
    row_sum, row_squares = lax.psum(
        (jnp.sum(in_float, axis=2), jnp.sum(in_float * in_float, axis=2)), "tensor"
    )
    row_mean = row_sum / D
    row_scale = lax.rsqrt(row_squares / D - row_mean * row_mean + norm_eps)
    centred = (in_float - row_mean[:, :, None]) * row_scale[:, :, None]
    normed = (centred * norm_gain).astype(jnp.bfloat16)
    normed_all = lax.all_gather(normed, "section", axis=1, tiled=True).reshape(flat_rows, width)
    grad_share = []
    kept_pre = []
    for way, step in enumerate((1, -1)):
        term = jnp.einsum(
            "rd,hd->rh",
            grad_all,
            down_weight[way * half : (way + 1) * half],
            preferred_element_type=jnp.float32,
        ).astype(jnp.bfloat16)
        grad_share.append(ring_reduce_scatter(term, step))
    for way, step in enumerate((1, -1)):
        term = jnp.dot(
            normed_all,
            up_weight[:, way * half : (way + 1) * half],
            preferred_element_type=jnp.float32,
        ).astype(jnp.bfloat16)
        kept_pre.append(ring_reduce_scatter(term, step))
    grad_pre = ring_gather(
        [(grad_share[way] * gelu_slope(kept_pre[way])).astype(jnp.bfloat16) for way in range(2)]
    )
    hidden = ring_gather([gelu_tanh(kept_pre[way]).astype(jnp.bfloat16) for way in range(2)])
    grad_normed = jnp.transpose(
        lax.psum_scatter(
            jnp.einsum(
                "mrh,dh->rmd",
                grad_pre.reshape(micro_count, row_total, hid_width),
                up_weight,
                preferred_element_type=jnp.float32,
            ).astype(jnp.bfloat16),
            "section",
            scatter_dimension=0,
            tiled=True,
        ).astype(jnp.float32),
        (1, 0, 2),
    )
    grad_up = jnp.dot(normed_all.T, grad_pre, preferred_element_type=jnp.float32).astype(
        jnp.bfloat16
    )
    out_terms = lax.psum_scatter(
        jnp.einsum(
            "mrh,hd->rmd",
            hidden.reshape(micro_count, row_total, hid_width),
            down_weight,
            preferred_element_type=jnp.float32,
        ).astype(jnp.bfloat16),
        "section",
        scatter_dimension=0,
        tiled=True,
    ).astype(jnp.float32)
    states = (in_float + jnp.transpose(out_terms, (1, 0, 2))).astype(jnp.bfloat16)
    grad_down = jnp.dot(hidden.T, grad_all, preferred_element_type=jnp.float32).astype(jnp.bfloat16)
    grad_gain = lax.psum(jnp.sum(grad_normed * centred, axis=(0, 1)), "section")
    grad_centred = grad_normed * norm_gain
    sum_first, sum_second = lax.psum(
        (jnp.sum(grad_centred, axis=2), jnp.sum(grad_centred * centred, axis=2)), "tensor"
    )
    correction = grad_centred - (sum_first / D)[:, :, None] - centred * (sum_second / D)[:, :, None]
    input_grads = (cotangent.astype(jnp.float32) + row_scale[:, :, None] * correction).astype(
        jnp.bfloat16
    )
    return (states, input_grads, grad_up, grad_down, grad_gain)


def solution(mesh):
    placed = (
        P(None, "section", "tensor"),
        P(None, "section", "tensor"),
        P("tensor", "section"),
        P("section", "tensor"),
        P("tensor"),
    )
    return jax.shard_map(
        per_device,
        mesh=mesh,
        in_specs=placed,
        out_specs=(
            P(None, "section", "tensor"),
            P(None, "section", "tensor"),
            P("tensor", "section"),
            P("section", "tensor"),
            P("tensor"),
        ),
        check_vma=False,
    )
```

```python
import jax
import jax.numpy as jnp
from jax import lax
from jax.sharding import PartitionSpec as P

D = 12288


norm_eps = 1e-05
gelu_c = 0.7978845608
cubic_c = 0.044715


def gelu_tanh(values):
    inner_arg = gelu_c * (values + cubic_c * values * values * values)
    return 0.5 * values * (1.0 + jnp.tanh(inner_arg))


def gelu_slope(values):
    tanh_value = jnp.tanh(gelu_c * (values + cubic_c * values * values * values))
    return 0.5 * (1.0 + tanh_value) + 0.5 * values * (1.0 - tanh_value * tanh_value) * gelu_c * (
        1.0 + 3.0 * cubic_c * values * values
    )


def ring_pairs(count, step):
    ring = list(range(0, count, 2)) + list(range(count - 1, 0, -2))
    return [(ring[i], ring[(i + step) % count]) for i in range(count)]


def ring_place(count):
    index = lax.axis_index("tensor")
    return jnp.where(index % 2 == 0, index // 2, count - 1 - index // 2)


def ring_reduce_scatter(partial, step):
    count = lax.axis_size("tensor")
    place = ring_place(count)
    rows = partial.shape[0] // count
    pairs = ring_pairs(count, step)

    def own(owner):
        owner = lax.rem(owner + 2 * count, count)
        return lax.dynamic_slice(partial, (owner * rows, 0), (rows, partial.shape[1]))

    held = own(place - step)
    for hop in range(count - 1):
        arrived = lax.ppermute(held, "tensor", pairs)
        total = arrived.astype(jnp.float32) + own(place - step * (2 + hop)).astype(jnp.float32)
        held = total.astype(jnp.bfloat16)
    return total


def swap(value, axis, bit):
    count = lax.axis_size(axis)
    return lax.ppermute(value, axis, [(i, i ^ bit) for i in range(count)])


def bits_of(axis):
    count = lax.axis_size(axis)
    bits = []
    bit = 1
    while bit < count:
        bits.append(bit)
        bit *= 2
    return bits


def butterfly_sum(value, axis):
    for bit in bits_of(axis):
        value = value + swap(value, axis, bit)
    return value


def section_gather(rows):
    for bit in reversed(bits_of("section")):
        rows = jnp.concatenate([rows, swap(rows, "section", bit)], axis=0)
    return rows


def section_sum(terms):
    total = terms
    for bit in bits_of("section"):
        near = terms.shape[0] // 2
        arrived = swap(terms[near:], "section", bit)
        total = terms[:near].astype(jnp.float32) + arrived.astype(jnp.float32)
        terms = total.astype(jnp.bfloat16)
    return total.astype(jnp.float32)


def ring_gather_pair(first, second, first_whole, second_whole, beside):
    count = lax.axis_size("tensor")
    lag = 3 * (count - 1) // 7
    place = ring_place(count)
    rows, half = first[0].shape
    wholes = [first_whole, second_whole]
    held = [list(first), list(second)]
    results = []

    def store(which, hop):
        for way, step in enumerate((1, -1)):
            owner = lax.rem(place - step * hop + count, count)
            wholes[which] = lax.dynamic_update_slice(
                wholes[which], held[which][way], (owner * rows, way * half)
            )

    def send(which):
        held[which] = [
            lax.ppermute(held[which][way], "tensor", ring_pairs(count, step))
            for way, step in enumerate((1, -1))
        ]

    store(0, 0)
    for turn in range(count - 1 + lag):
        if turn == lag:
            joined = lax.optimization_barrier((tuple(held[0]), tuple(held[1])))
            held = [list(joined[0]), list(joined[1])]
            store(1, 0)
        if turn < count - 1:
            send(0)
            store(0, turn + 1)
        if turn >= lag:
            send(1)
            late = turn - (count - 1)
            if 0 <= late < len(beside):
                made = beside[late](wholes[0])
                joined, made = lax.optimization_barrier((tuple(held[1]), made))
                held[1] = list(joined)
                results.append(made)
            store(1, turn - lag + 1)
    return wholes[1], results


def per_device(inputs, cotangent, up_weight, down_weight, norm_gain):
    micro_count, local_rows, width = inputs.shape
    hid_width = up_weight.shape[1]
    half = hid_width // 2
    own_rows = micro_count * local_rows
    grad_own = cotangent.reshape(own_rows, width)
    grad_all = section_gather(grad_own)
    in_float = inputs.reshape(own_rows, width).astype(jnp.float32)
    row_sums = jnp.stack([jnp.sum(in_float, axis=1), jnp.sum(in_float * in_float, axis=1)])
    grad_all, row_sums = lax.optimization_barrier((grad_all, row_sums))
    row_sum, row_squares = butterfly_sum(row_sums, "tensor")
    row_mean = row_sum / D
    row_scale = lax.rsqrt(row_squares / D - row_mean * row_mean + norm_eps)
    centred = (in_float - row_mean[:, None]) * row_scale[:, None]
    normed = (centred * norm_gain).astype(jnp.bfloat16)
    normed_all = section_gather(normed)
    grad_share = []
    kept_pre = []
    for way, step in enumerate((1, -1)):
        term = jnp.einsum(
            "rd,hd->rh",
            grad_all,
            down_weight[way * half : (way + 1) * half],
            preferred_element_type=jnp.float32,
        ).astype(jnp.bfloat16)
        grad_share.append(ring_reduce_scatter(term, step))
    for way, step in enumerate((1, -1)):
        term = jnp.dot(
            normed_all,
            up_weight[:, way * half : (way + 1) * half],
            preferred_element_type=jnp.float32,
        ).astype(jnp.bfloat16)
        kept_pre.append(ring_reduce_scatter(term, step))
    blank = jnp.zeros((normed_all.shape[0], hid_width), jnp.bfloat16)

    def normed_product(grad_pre):
        return jnp.einsum("rh,dh->rd", grad_pre, up_weight, preferred_element_type=jnp.float32).astype(
            jnp.bfloat16
        )

    def up_product(grad_pre):
        return jnp.dot(normed_all.T, grad_pre, preferred_element_type=jnp.float32).astype(
            jnp.bfloat16
        )

    hidden, (normed_term, grad_up) = ring_gather_pair(
        [(grad_share[way] * gelu_slope(kept_pre[way])).astype(jnp.bfloat16) for way in range(2)],
        [gelu_tanh(kept_pre[way]).astype(jnp.bfloat16) for way in range(2)],
        blank,
        blank,
        (normed_product, up_product),
    )
    grad_normed = section_sum(normed_term)
    out_terms = section_sum(
        jnp.dot(hidden, down_weight, preferred_element_type=jnp.float32).astype(jnp.bfloat16)
    )
    states = (in_float + out_terms).astype(jnp.bfloat16).reshape(inputs.shape)
    grad_down = jnp.dot(hidden.T, grad_all, preferred_element_type=jnp.float32).astype(jnp.bfloat16)
    grad_gain = butterfly_sum(jnp.sum(grad_normed * centred, axis=0), "section")
    grad_centred = grad_normed * norm_gain
    sum_first, sum_second = butterfly_sum(
        jnp.stack([jnp.sum(grad_centred, axis=1), jnp.sum(grad_centred * centred, axis=1)]),
        "tensor",
    )
    correction = grad_centred - (sum_first / D)[:, None] - centred * (sum_second / D)[:, None]
    input_grads = (grad_own.astype(jnp.float32) + row_scale[:, None] * correction).astype(
        jnp.bfloat16
    )
    return (states, input_grads.reshape(inputs.shape), grad_up, grad_down, grad_gain)


def solution(mesh):
    placed = (
        P(None, "section", "tensor"),
        P(None, "section", "tensor"),
        P("tensor", "section"),
        P("section", "tensor"),
        P("tensor"),
    )
    return jax.shard_map(
        per_device,
        mesh=mesh,
        in_specs=placed,
        out_specs=(
            P(None, "section", "tensor"),
            P(None, "section", "tensor"),
            P("tensor", "section"),
            P("section", "tensor"),
            P("tensor"),
        ),
        check_vma=False,
    )
```

```python
import jax
import jax.numpy as jnp
from jax import lax
from jax.sharding import PartitionSpec as P

D = 12288


norm_eps = 1e-05
gelu_c = 0.7978845608
cubic_c = 0.044715


def gelu_tanh(values):
    inner_arg = gelu_c * (values + cubic_c * values * values * values)
    return 0.5 * values * (1.0 + jnp.tanh(inner_arg))


def gelu_slope(values):
    tanh_value = jnp.tanh(gelu_c * (values + cubic_c * values * values * values))
    return 0.5 * (1.0 + tanh_value) + 0.5 * values * (1.0 - tanh_value * tanh_value) * gelu_c * (
        1.0 + 3.0 * cubic_c * values * values
    )


def ring_pairs(count, step):
    ring = list(range(0, count, 2)) + list(range(count - 1, 0, -2))
    return [(ring[i], ring[(i + step) % count]) for i in range(count)]


def ring_place(count):
    index = lax.axis_index("tensor")
    return jnp.where(index % 2 == 0, index // 2, count - 1 - index // 2)


def ring_reduce_scatter(partial, step):
    count = lax.axis_size("tensor")
    place = ring_place(count)
    rows = partial.shape[0] // count
    pairs = ring_pairs(count, step)

    def own(owner):
        owner = lax.rem(owner + 2 * count, count)
        return lax.dynamic_slice(partial, (owner * rows, 0), (rows, partial.shape[1]))

    held = own(place - step)
    for hop in range(count - 1):
        arrived = lax.ppermute(held, "tensor", pairs)
        total = arrived.astype(jnp.float32) + own(place - step * (2 + hop)).astype(jnp.float32)
        held = total.astype(jnp.bfloat16)
    return total


def swap(value, axis, bit):
    count = lax.axis_size(axis)
    return lax.ppermute(value, axis, [(i, i ^ bit) for i in range(count)])


def bits_of(axis):
    count = lax.axis_size(axis)
    bits = []
    bit = 1
    while bit < count:
        bits.append(bit)
        bit *= 2
    return bits


def butterfly_sum(value, axis):
    for bit in bits_of(axis):
        value = value + swap(value, axis, bit)
    return value


def section_gather(rows):
    for bit in reversed(bits_of("section")):
        rows = jnp.concatenate([rows, swap(rows, "section", bit)], axis=0)
    return rows


def section_sum(terms):
    total = terms
    for bit in bits_of("section"):
        near = terms.shape[0] // 2
        arrived = swap(terms[near:], "section", bit)
        total = terms[:near].astype(jnp.float32) + arrived.astype(jnp.float32)
        terms = total.astype(jnp.bfloat16)
    return total.astype(jnp.float32)


def ring_gather_pair(first, second, first_whole, second_whole, beside):
    count = lax.axis_size("tensor")
    lag = max(1, (count - 1) // 7)
    place = ring_place(count)
    rows, half = first[0].shape
    wholes = [first_whole, second_whole]
    held = [list(first), list(second)]
    results = []

    def store(which, hop):
        for way, step in enumerate((1, -1)):
            owner = lax.rem(place - step * hop + count, count)
            wholes[which] = lax.dynamic_update_slice(
                wholes[which], held[which][way], (owner * rows, way * half)
            )

    def send(which):
        held[which] = [
            lax.ppermute(held[which][way], "tensor", ring_pairs(count, step))
            for way, step in enumerate((1, -1))
        ]

    store(0, 0)
    for turn in range(count - 1 + lag):
        if turn == lag:
            joined = lax.optimization_barrier((tuple(held[0]), tuple(held[1])))
            held = [list(joined[0]), list(joined[1])]
            store(1, 0)
        if turn < count - 1:
            send(0)
            store(0, turn + 1)
        if turn >= lag:
            send(1)
            if turn == count - 1:
                results = [product(wholes[0]) for product in beside]
                joined, _ = lax.optimization_barrier((tuple(held[1]), tuple(results)))
                held[1] = list(joined)
            store(1, turn - lag + 1)
    return wholes[1], results


def per_device(inputs, cotangent, up_weight, down_weight, norm_gain):
    micro_count, local_rows, width = inputs.shape
    hid_width = up_weight.shape[1]
    half = hid_width // 2
    own_rows = micro_count * local_rows
    grad_own = cotangent.reshape(own_rows, width)
    grad_all = section_gather(grad_own)
    in_float = inputs.reshape(own_rows, width).astype(jnp.float32)
    row_sums = jnp.stack([jnp.sum(in_float, axis=1), jnp.sum(in_float * in_float, axis=1)])
    grad_all, row_sums = lax.optimization_barrier((grad_all, row_sums))
    row_sum, row_squares = butterfly_sum(row_sums, "tensor")
    row_mean = row_sum / D
    row_scale = lax.rsqrt(row_squares / D - row_mean * row_mean + norm_eps)
    centred = (in_float - row_mean[:, None]) * row_scale[:, None]
    normed = (centred * norm_gain).astype(jnp.bfloat16)
    normed_all = section_gather(normed)
    grad_share = []
    kept_pre = []
    for way, step in enumerate((1, -1)):
        term = jnp.einsum(
            "rd,hd->rh",
            grad_all,
            down_weight[way * half : (way + 1) * half],
            preferred_element_type=jnp.float32,
        ).astype(jnp.bfloat16)
        grad_share.append(ring_reduce_scatter(term, step))
    for way, step in enumerate((1, -1)):
        term = jnp.dot(
            normed_all,
            up_weight[:, way * half : (way + 1) * half],
            preferred_element_type=jnp.float32,
        ).astype(jnp.bfloat16)
        kept_pre.append(ring_reduce_scatter(term, step))
    blank = jnp.zeros((normed_all.shape[0], hid_width), jnp.bfloat16)

    def normed_product(grad_pre):
        return jnp.einsum("rh,dh->rd", grad_pre, up_weight, preferred_element_type=jnp.float32).astype(
            jnp.bfloat16
        )

    def up_product(grad_pre):
        return jnp.dot(normed_all.T, grad_pre, preferred_element_type=jnp.float32).astype(
            jnp.bfloat16
        )

    hidden, (normed_term, grad_up) = ring_gather_pair(
        [(grad_share[way] * gelu_slope(kept_pre[way])).astype(jnp.bfloat16) for way in range(2)],
        [gelu_tanh(kept_pre[way]).astype(jnp.bfloat16) for way in range(2)],
        blank,
        blank,
        (normed_product, up_product),
    )
    grad_normed = section_sum(normed_term)
    out_terms = section_sum(
        jnp.dot(hidden, down_weight, preferred_element_type=jnp.float32).astype(jnp.bfloat16)
    )
    states = (in_float + out_terms).astype(jnp.bfloat16).reshape(inputs.shape)
    grad_down = jnp.dot(hidden.T, grad_all, preferred_element_type=jnp.float32).astype(jnp.bfloat16)
    grad_gain = butterfly_sum(jnp.sum(grad_normed * centred, axis=0), "section")
    grad_centred = grad_normed * norm_gain
    sum_first, sum_second = butterfly_sum(
        jnp.stack([jnp.sum(grad_centred, axis=1), jnp.sum(grad_centred * centred, axis=1)]),
        "tensor",
    )
    correction = grad_centred - (sum_first / D)[:, None] - centred * (sum_second / D)[:, None]
    input_grads = (grad_own.astype(jnp.float32) + row_scale[:, None] * correction).astype(
        jnp.bfloat16
    )
    return (states, input_grads.reshape(inputs.shape), grad_up, grad_down, grad_gain)


def solution(mesh):
    placed = (
        P(None, "section", "tensor"),
        P(None, "section", "tensor"),
        P("tensor", "section"),
        P("section", "tensor"),
        P("tensor"),
    )
    return jax.shard_map(
        per_device,
        mesh=mesh,
        in_specs=placed,
        out_specs=(
            P(None, "section", "tensor"),
            P(None, "section", "tensor"),
            P("tensor", "section"),
            P("section", "tensor"),
            P("tensor"),
        ),
        check_vma=False,
    )
```
